256 devices in a mesh: items: 128 (over z, x, y_hi, core), rep: 2 (over y_lo).
Axes of the slice: x: 4, y: 4 (y_hi: 2, y_lo: 2; y = y_hi * 2 + y_lo), z: 8, core: 2. Of those that a mesh axis runs over, the one named last changes fastest.
Arguments:
- teacher_queries: bfloat16 [262144, 1024], P(('items', 'rep')), may hold values from -6 to 6
- teacher_items: bfloat16 [65536, 1024], P('items'), may hold values from -6 to 6
- student_queries: bfloat16 [262144, 128], P(('items', 'rep')), may hold values from -6 to 6
- student_items: bfloat16 [65536, 128], P('items'), may hold values from -6 to 6
- block_mask: int32 [4096, 7], P(('items', 'rep')), may hold values from 0 to 1, as said below
- pass_index: int32 [262144], P(('items', 'rep')), may hold values from 0 to 3
- teacher_norms: float32 [4, 262144], P(None, ('items', 'rep')), may hold values from 8 to 10
- student_norms: float32 [4, 262144], P(None, ('items', 'rep')), may hold values from 8 to 10
Outputs:
- query_grad: float32 [262144, 128], P(('items', 'rep'))
- item_grad: float32 [65536, 128], P(('items', 'rep'))
The draws below stay inside these ranges and needn't reach their ends.
Inputs may be any that keep to these rules, and one draw needn't show every extreme that they name: block_mask[b, o] is 1 where the requests of block b visit the span at offset o - 3 from their own span, else 0; a block visits at most 5 of the 7 offsets.
All inputs are finite; a program needn't handle non-finite values.
Results may differ from the reference program's by a relative error of at most 0.0026.
Values may be sent and summed in bfloat16 or wider, within the bound.
No kernel may reach another device: no remote copies, remote signals or barrier semaphores. Data moves between devices by JAX's collectives and lax.ppermute only.
A program may use at most 64 MiB of HBM per device.

```python
import math
import jax
import jax.numpy as jnp
from jax import lax

DT = 1024
DS = 128
REACH = 3
PASSES = 4
RB = 64
REQ_DEV = 1024
SPAN = 512
VISITS = 7
BLOCKS_DEV = 16
BLOCKS = 4096
REQ = 262144
ITEMS = 65536
N_ITEMS = 128
N_REP = 2


def draw_block_mask(key, part):
    key = jax.random.fold_in(key, 11)
    level_key, count_key, score_key, pick_key = jax.random.split(key, 4)
    groups = BLOCKS // BLOCKS_DEV
    levels = jax.random.randint(level_key, (groups,), 2, 6)
    row_levels = jnp.repeat(levels, BLOCKS_DEV)
    counts = jax.random.randint(count_key, (BLOCKS,), 1, 6)
    counts = jnp.minimum(counts, row_levels)
    chosen = jax.random.randint(pick_key, (), 0, BLOCKS)
    counts = jnp.where(jnp.arange(BLOCKS, dtype=jnp.int32) == chosen, 5, counts)
    raw = jax.random.randint(score_key, (BLOCKS, VISITS), 0, 1048576)
    scores = raw * VISITS + jnp.arange(VISITS, dtype=jnp.int32)[None, :]
    order = jnp.argsort(scores, axis=1, stable=True)
    ranks = jnp.argsort(order, axis=1, stable=True).astype(jnp.int32)
    return (ranks < counts[:, None]).astype(jnp.int32)


def with_ends(drawn, stream_key, low, top_value):
    index_at = [jax.random.randint(jax.random.fold_in(stream_key, axis), (), 0, length) for axis, length in enumerate(drawn.shape)]
    longest = drawn.shape.index(max(drawn.shape))
    beside = index_at[:longest] + [(index_at[longest] + 1) % drawn.shape[longest]] + index_at[longest + 1:]
    return drawn.at[tuple(index_at)].set(low).at[tuple(beside)].set(top_value)


def block_scale(stream_key, dims, pieces, least, top_value):
    loudness = 1.0
    for position, shards_of in pieces:
        draws = jax.random.uniform(jax.random.fold_in(jax.random.fold_in(stream_key, 6), position), (shards_of,), jnp.float32, least / len(pieces), top_value / len(pieces))
        loudness = loudness * jnp.repeat(jnp.exp(draws), dims[position] // shards_of).reshape((-1,) + (1,) * (len(dims) - 1 - position))
    return loudness


def centred(own_key, extent, spread, reach, cuts=(), kind=jnp.bfloat16):
    result = jax.random.normal(own_key, extent, jnp.float32) * spread
    if len(cuts) > 0:
        result = block_scale(own_key, extent, cuts, -0.22, 0.18) * result
    return jnp.clip(result, min=-reach, max=reach).astype(kind)


def setup_inputs(seed: int = 0) -> dict:
    arg_keys = jax.random.split(jax.random.key(seed), 9)
    teacher_queries = centred(arg_keys[0], (REQ, DT), 1.0, 6.0, ((0, 256),))
    teacher_items = centred(arg_keys[1], (ITEMS, DT), 1.0, 6.0, ((0, 128),))
    student_queries = centred(arg_keys[2], (REQ, DS), 1.0, 6.0, ((0, 256),))
    student_items = centred(arg_keys[3], (ITEMS, DS), 1.0, 6.0, ((0, 128),))
    block_mask = draw_block_mask(jax.random.fold_in(arg_keys[8], 71), 0)
    pass_index = with_ends(jax.random.randint(arg_keys[5], (REQ,), 0, PASSES), jax.random.fold_in(arg_keys[5], 1), 0, PASSES - 1).astype(jnp.int32)
    teacher_norms = jnp.clip(8.0 + 2.0 * jax.random.uniform(arg_keys[6], (PASSES, REQ), jnp.float32) ** block_scale(arg_keys[6], (PASSES, REQ), ((1, 256),), -0.2, 0.2), 8.0, 10.0)
    student_norms = jnp.clip(8.0 + 2.0 * jax.random.uniform(arg_keys[7], (PASSES, REQ), jnp.float32) ** block_scale(arg_keys[7], (PASSES, REQ), ((1, 256),), -0.2, 0.2), 8.0, 10.0)
    return dict(teacher_queries=teacher_queries, teacher_items=teacher_items, student_queries=student_queries, student_items=student_items, block_mask=block_mask, pass_index=pass_index, teacher_norms=teacher_norms, student_norms=student_norms)


logit_cap = 10.0
score_gain = 3.0
loss_weight = 8.0

def pair_gradient(t_raw, s_raw, z_teacher, z_student, weight, teacher_scale, student_scale):
    teacher = logit_cap * jnp.tanh(t_raw * (teacher_scale / logit_cap))
    student = logit_cap * jnp.tanh(s_raw * (student_scale / logit_cap))
    slope = 1.0 - (student / logit_cap) ** 2
    diff = jnp.exp(student - z_student[:, None]) - jnp.exp(teacher - z_teacher[:, None])
    grads = loss_weight * student_scale * weight[:, None] * diff * slope
    return grads.astype(jnp.bfloat16)

def reference(teacher_queries, teacher_items, student_queries, student_items, block_mask, pass_index, teacher_norms, student_norms):
    passes = jnp.arange(PASSES, dtype=jnp.int32)
    picked = (pass_index[None, :] == passes[:, None]).astype(jnp.float32)
    z_teacher_all = lax.optimization_barrier(jnp.sum(teacher_norms * picked, axis=0))
    z_student_all = lax.optimization_barrier(jnp.sum(student_norms * picked, axis=0))
    row_weights = jnp.repeat(block_mask.astype(jnp.float32), RB, axis=0)
    teacher_scale = score_gain / math.sqrt(DT)
    student_scale = score_gain / math.sqrt(DS)
    groups = N_ITEMS * N_REP

    def step(grads, group):
        start = group * REQ_DEV
        q_teacher = lax.dynamic_slice_in_dim(teacher_queries, start, REQ_DEV, 0)
        q_student = lax.dynamic_slice_in_dim(student_queries, start, REQ_DEV, 0)
        z_teacher = lax.dynamic_slice_in_dim(z_teacher_all, start, REQ_DEV, 0)
        z_student = lax.dynamic_slice_in_dim(z_student_all, start, REQ_DEV, 0)
        weights = lax.dynamic_slice_in_dim(row_weights, start, REQ_DEV, 0)
        owner = group // N_REP
        query_part = jnp.zeros((REQ_DEV, DS), jnp.float32)
        for offset in range(-REACH, REACH + 1):
            first = ((owner + offset) % N_ITEMS * SPAN).astype(jnp.int32)
            e_teacher = lax.dynamic_slice_in_dim(teacher_items, first, SPAN, 0)
            e_student = lax.dynamic_slice_in_dim(student_items, first, SPAN, 0)
            t_raw = jnp.dot(q_teacher, e_teacher.T, preferred_element_type=jnp.float32)
            s_raw = jnp.dot(q_student, e_student.T, preferred_element_type=jnp.float32)
            grad_pair = pair_gradient(t_raw, s_raw, z_teacher, z_student, weights[:, offset + REACH], teacher_scale, student_scale)
            query_part = query_part + jnp.dot(grad_pair, e_student, preferred_element_type=jnp.float32)
            item_part = jnp.dot(grad_pair.T, q_student, preferred_element_type=jnp.float32)
            current = lax.dynamic_slice_in_dim(grads, first, SPAN, 0)
            grads = lax.dynamic_update_slice_in_dim(grads, current + item_part, first, 0)
        return (grads, query_part)
    grads, query_parts = lax.scan(step, jnp.zeros((ITEMS, DS), jnp.float32), jnp.arange(groups, dtype=jnp.int32))
    return (query_parts.reshape(REQ, DS), grads)
```

```python
import functools
import math

import jax
import jax.numpy as jnp
from jax import lax
from jax.experimental import pallas as pl
from jax.experimental.pallas import tpu as pltpu
from jax.sharding import PartitionSpec as P

logit_cap = 10.0
score_gain = 3.0
loss_weight = 8.0
log2e = 1.0 / math.log(2.0)
never = 1e9
AXES = ("items", "rep")


def edges(n_items, move):
    pairs = []
    for flat in range(n_items * 2):
        item, rep = flat // 2, flat % 2
        pos, y, core = item // 4, (item // 2 % 2) * 2 + rep, item % 2
        pos, y, core = move(pos, y, core)
        pos = pos % (n_items // 4)
        target = ((pos * 2 + y // 2) * 2 + core) * 2 + y % 2
        pairs.append((flat, target))
    return pairs


def step(y):
    return -1 if y < 2 else 1


def far(p, y, c):
    return (p + 1, y, 0) if c == 1 else (p - 1, y, 1)


def relay_one(p, y, c):
    if y < 2:
        return (p + 1, y, 0) if c == 0 else (p, 3 - y, 0)
    return (p - 1, y, 1) if c == 1 else (p, 3 - y, 1)


def relay_two(p, y, c):
    if y < 2:
        return (p + 1, y, 0) if c == 0 else (p, y ^ 1, 1)
    return (p - 1, y, 1) if c == 1 else (p, y ^ 1, 0)


def cross(p, y, c):
    return p, 3 - y, c


def pair(p, y, c):
    return p, y ^ 1, c


def two(p, y, c):
    return p, y ^ 2, c


def core(p, y, c):
    return p, y, 1 - c


def diag(p, y, c):
    return p + step(y), 3 - y, c


def diag_two(p, y, c):
    return p + step(y), y ^ 2, c


def diag_two_core(p, y, c):
    return p + step(y), y ^ 2, 1 - c


def visit_kernel(row, first, scales, zt_ref, zs_ref, tq_ref, sqt_ref, sq_ref, piece_ref, *refs):
    q_ref, term_ref = refs[-2:]
    width = tq_ref.shape[0]
    teacher = piece_ref[:, :width]
    student = piece_ref[:, width:]
    t_raw = jnp.dot(teacher, tq_ref[...], preferred_element_type=jnp.float32)
    s_raw = jnp.dot(student, sqt_ref[...], preferred_element_type=jnp.float32)
    t_tanh = jnp.tanh(t_raw * scales[0])
    s_tanh = jnp.tanh(s_raw * scales[1])
    t_exp = jnp.exp2(t_tanh * (logit_cap * log2e) - zt_ref[row : row + 1, :])
    s_exp = jnp.exp2(s_tanh * (logit_cap * log2e) - zs_ref[row : row + 1, :])
    grads = ((s_exp - t_exp) * (1.0 - s_tanh * s_tanh)).astype(jnp.bfloat16)
    term_ref[...] = jnp.dot(grads, sq_ref[...], preferred_element_type=jnp.float32)
    q_part = lax.dot_general(
        student, grads, (((0,), (0,)), ((), ())), preferred_element_type=jnp.float32
    )
    q_ref[...] = q_part if first else refs[0][...] + q_part


def visit(row, shared, scales, piece, q):
    rows, width = piece.shape[0], shared[4].shape[1]
    requests = shared[4].shape[0]
    vmem = pl.BlockSpec(memory_space=pltpu.VMEM)
    operands = (*shared, piece) if q is None else (*shared, piece, q)
    return pl.pallas_call(
        functools.partial(visit_kernel, row, q is None, scales),
        out_shape=(
            jax.ShapeDtypeStruct((width, requests), jnp.float32),
            jax.ShapeDtypeStruct((rows, width), jnp.float32),
        ),
        in_specs=[vmem] * len(operands),
        out_specs=(vmem, vmem),
        compiler_params=pltpu.CompilerParams(vmem_limit_bytes=24 << 20),
    )(*operands)


def shards(
    teacher_queries,
    teacher_items,
    student_queries,
    student_items,
    block_mask,
    pass_index,
    teacher_norms,
    student_norms,
):
    n_items = lax.axis_size("items")
    rows = teacher_queries.shape[0]
    blocks = block_mask.shape[0]
    span = teacher_items.shape[0]
    half = span // 2
    quarter = half // 2
    teacher_scale = score_gain / math.sqrt(teacher_queries.shape[1])
    student_scale = score_gain / math.sqrt(student_queries.shape[1])
    scales = (teacher_scale / logit_cap, student_scale / logit_cap)

    item = lax.axis_index("items")
    rep = lax.axis_index("rep")
    core_id = item % 2
    type_b = item // 2 % 2

    def send(block, move):
        return lax.ppermute(block, AXES, edges(n_items, move))

    mine = rep * half
    own_half = jnp.concatenate(
        [
            lax.dynamic_slice_in_dim(teacher_items, mine, half, 0),
            lax.dynamic_slice_in_dim(student_items, mine, half, 0),
        ],
        axis=1,
    )
    cross_a = send(own_half[:quarter], cross)
    cross_b = send(own_half[quarter:], cross)
    own = jnp.concatenate([teacher_items, student_items], axis=1)
    far_span = send(own, far)
    core_span = send(own, core)

    passes = jnp.arange(teacher_norms.shape[0], dtype=jnp.int32)
    picked = (pass_index[None, :] == passes[:, None]).astype(jnp.float32)
    fold = math.log2(loss_weight * student_scale)
    zt = jnp.sum(teacher_norms * picked, axis=0) * log2e - fold
    zs = jnp.sum(student_norms * picked, axis=0) * log2e - fold
    near = 1 - 2 * core_id
    ahead = 2 - 4 * type_b
    offsets = jnp.stack([0 * near, near, -3 * near, ahead, ahead + near, -ahead, near - ahead])
    reach = block_mask.shape[1] // 2
    chosen = offsets[:, None, None] + reach == jnp.arange(2 * reach + 1)[None, None, :]
    on = jnp.any(chosen & (block_mask[None] != 0), axis=2)
    on = jnp.broadcast_to(on[:, :, None], (on.shape[0], blocks, rows // blocks))
    on = on.reshape(on.shape[0], rows)
    shared = (
        jnp.where(on, zt[None], never),
        jnp.where(on, zs[None], never),
        teacher_queries.T,
        student_queries.T,
        student_queries,
    )

    q, own_term = visit(0, shared, scales, own, None)
    q, core_term = visit(1, shared, scales, core_span, q)

    pair_a = send(cross_a, pair)
    pair_b = send(cross_b, pair)
    cross_half = jnp.concatenate([cross_a, cross_b])
    pair_half = jnp.concatenate([pair_a, pair_b])
    relays = jnp.logical_xor(type_b == 0, core_id == 1)
    far_half = lax.dynamic_slice_in_dim(far_span, mine, half, 0)
    next_one = send(jnp.where(relays, cross_half, far_half), relay_one)
    next_two = send(jnp.where(relays, pair_half, next_one), relay_two)

    q, far_term = visit(2, shared, scales, far_span, q)
    far_back = send(far_term, far)
    across = jnp.concatenate([cross_half, pair_half])
    across_core = send(across, core)
    q, across_term = visit(3, shared, scales, across, q)
    q, across_core_term = visit(4, shared, scales, across_core, q)
    next_one_core = send(next_one, core)
    q, one_term = visit(5, shared, scales, next_one, q)
    q, one_core_term = visit(6, shared, scales, next_one_core, q)
    swapped = send(jnp.concatenate([core_term, across_core_term, one_core_term]), core)
    own_total = own_term + far_back + swapped[:span]
    across_total = across_term + swapped[span : 2 * span]
    one_total = one_term + swapped[2 * span :]
    pair_back = send(lax.dynamic_slice_in_dim(own_total, half - mine, half, 0), pair)
    cross_back = send(across_total[:half], cross)
    two_back = send(across_total[half:], two)
    one_back = send(one_total, diag)
    total = lax.dynamic_slice_in_dim(own_total, mine, half, 0)
    total = total + pair_back + cross_back + two_back + one_back

    next_two_core = send(next_two, core)
    q, two_term = visit(5, shared, scales, next_two, q)
    last_back = send(two_term, diag_two)
    q, two_core_term = visit(6, shared, scales, next_two_core, q)
    last_core_back = send(two_core_term, diag_two_core)
    return q.T, total + last_back + last_core_back


def solution(mesh):
    return jax.shard_map(
        shards,
        mesh=mesh,
        in_specs=(
            P(("items", "rep"), None),
            P("items", None),
            P(("items", "rep"), None),
            P("items", None),
            P(("items", "rep"), None),
            P(("items", "rep")),
            P(None, ("items", "rep")),
            P(None, ("items", "rep")),
        ),
        out_specs=(P(("items", "rep"), None), P(("items", "rep"), None)),
        check_vma=False,
    )
```

```python
import functools
import math

import jax
import jax.numpy as jnp
from jax import lax
from jax.experimental import pallas as pl
from jax.experimental.pallas import tpu as pltpu
from jax.sharding import PartitionSpec as P

logit_cap = 10.0
score_gain = 3.0
loss_weight = 8.0
log2e = 1.0 / math.log(2.0)
never = 1e9
long_cost = 10**10
AXES = ("items", "rep")


def edges(n_items, move):
    pairs = []
    for flat in range(n_items * 2):
        item, rep = flat // 2, flat % 2
        pos, y, core = item // 4, (item // 2 % 2) * 2 + rep, item % 2
        pos, y, core = move(pos, y, core)
        pos = pos % (n_items // 4)
        target = ((pos * 2 + y // 2) * 2 + core) * 2 + y % 2
        pairs.append((flat, target))
    return pairs


def step(y):
    return -1 if y < 2 else 1


def far(p, y, c):
    return (p + 1, y, 0) if c == 1 else (p - 1, y, 1)


def cross(p, y, c):
    return p, 3 - y, c


def pair(p, y, c):
    return p, y ^ 1, c


def two(p, y, c):
    return p, y ^ 2, c


def core(p, y, c):
    return p, y, 1 - c


def diag(p, y, c):
    return p + step(y), 3 - y, c


def diag_two(p, y, c):
    return p + step(y), y ^ 2, c


def far_pair(p, y, c):
    p, y, c = far(p, y, c)
    return p, y ^ 1, c


def gather_kernel(rep_ref, teacher_ref, student_ref, out_ref, sems):
    rows = out_ref.shape[0]
    part = pl.ds(pl.multiple_of(rep_ref[0] * rows, rows), rows)
    copies = []
    for source, first in ((teacher_ref, 0), (student_ref, teacher_ref.shape[1])):
        target = out_ref.at[:, pl.ds(first, source.shape[1])]
        copies.append(pltpu.make_async_copy(source.at[part, :], target, sems.at[len(copies)]))
    for copy in copies:
        copy.start()
    for copy in copies:
        copy.wait()


def gather(rep, teacher, student):
    rows, width = teacher.shape[0] // 2, teacher.shape[1] + student.shape[1]
    whole = pl.BlockSpec(memory_space=pl.ANY)
    return pl.pallas_call(
        gather_kernel,
        out_shape=jax.ShapeDtypeStruct((rows, width), teacher.dtype),
        in_specs=[pl.BlockSpec(memory_space=pltpu.SMEM), whole, whole],
        out_specs=pl.BlockSpec(memory_space=pltpu.VMEM),
        scratch_shapes=[pltpu.SemaphoreType.DMA((2,))],
        compiler_params=pltpu.CompilerParams(vmem_limit_bytes=56 << 20),
        cost_estimate=pl.CostEstimate(flops=1, bytes_accessed=1, transcendentals=0),
    )(rep, teacher, student)


def turn_kernel(tq_ref, sq_ref, tqt_ref, sqt_ref):
    rows = 256
    for start in range(0, tq_ref.shape[0], rows):
        tqt_ref[:, start : start + rows] = tq_ref[start : start + rows, :].T
        sqt_ref[:, start : start + rows] = sq_ref[start : start + rows, :].T


def turn(tq, sq):
    vmem = pl.BlockSpec(memory_space=pltpu.VMEM)
    return pl.pallas_call(
        turn_kernel,
        out_shape=tuple(pltpu.VMEM(block.shape[::-1], block.dtype) for block in (tq, sq)),
        in_specs=[vmem] * 2,
        out_specs=(vmem,) * 2,
        compiler_params=pltpu.CompilerParams(vmem_limit_bytes=16 << 20),
        cost_estimate=pl.CostEstimate(flops=1, bytes_accessed=1, transcendentals=0),
    )(tq, sq)


def visit_kernel(parts, rows, first, scales, rep_ref, *refs):
    groups = len(rows)
    term_ref = refs[-1]
    if parts is None:
        width = refs[0].shape[1] - term_ref.shape[1]
        teacher, student = refs[0][:, :width], refs[0][:, width:]
        refs = refs[1:]
    else:
        half = refs[0].shape[0] // 2
        rep = rep_ref[0]
        picks = [pl.ds(pl.multiple_of((1 - rep if part else rep) * half, half), half) for part in parts]
        teacher, student = (
            jnp.concatenate([ref[pick, :] for pick in picks]) if len(picks) > 1 else ref[picks[0], :]
            for ref in refs[:2]
        )
        refs = refs[2:]
    term = None
    for group, row in enumerate(rows):
        zt_ref, zs_ref, tqt_ref, sqt_ref, sq_ref = refs[group * 5 : group * 5 + 5]
        t_raw = jnp.dot(teacher, tqt_ref[...], preferred_element_type=jnp.float32)
        s_raw = jnp.dot(student, sqt_ref[...], preferred_element_type=jnp.float32)
        t_tanh = jnp.tanh(t_raw * scales[0])
        s_tanh = jnp.tanh(s_raw * scales[1])
        t_exp = jnp.exp2(t_tanh * (logit_cap * log2e) - zt_ref[row : row + 1, :])
        s_exp = jnp.exp2(s_tanh * (logit_cap * log2e) - zs_ref[row : row + 1, :])
        grads = ((s_exp - t_exp) * (1.0 - s_tanh * s_tanh)).astype(jnp.bfloat16)
        part = jnp.dot(grads, sq_ref[...], preferred_element_type=jnp.float32)
        term = part if term is None else term + part
        q_part = lax.dot_general(
            student, grads, (((0,), (0,)), ((), ())), preferred_element_type=jnp.float32
        )
        q_ref = refs[-1 - groups + group]
        q_ref[...] = q_part if first else refs[groups * 5 + group][...] + q_part
    term_ref[...] = term


def visit(rep, piece, parts, rows, groups, scales, totals, cost=1):
    width, requests = groups[0][3].shape
    vmem = pl.BlockSpec(memory_space=pltpu.VMEM)
    items = piece[0].shape[0] if parts is None else piece[0].shape[0] // 2 * len(parts)
    operands = [*piece]
    for group in groups:
        operands.extend(group)
    operands.extend(totals)
    *totals, term = pl.pallas_call(
        functools.partial(visit_kernel, parts, rows, not totals, scales),
        out_shape=tuple([jax.ShapeDtypeStruct((width, requests), jnp.float32)] * len(groups))
        + (jax.ShapeDtypeStruct((items, width), jnp.float32),),
        in_specs=[pl.BlockSpec(memory_space=pltpu.SMEM)] + [vmem] * len(operands),
        out_specs=(vmem,) * (len(groups) + 1),
        compiler_params=pltpu.CompilerParams(vmem_limit_bytes=24 << 20),
        cost_estimate=pl.CostEstimate(flops=cost, bytes_accessed=1, transcendentals=0),
    )(rep, *operands)
    return totals, term


def shards(
    teacher_queries,
    teacher_items,
    student_queries,
    student_items,
    block_mask,
    pass_index,
    teacher_norms,
    student_norms,
):
    n_items = lax.axis_size("items")
    rows = teacher_queries.shape[0]
    blocks = block_mask.shape[0]
    span = teacher_items.shape[0]
    half = span // 2
    teacher_scale = score_gain / math.sqrt(teacher_queries.shape[1])
    student_scale = score_gain / math.sqrt(student_queries.shape[1])
    scales = (teacher_scale / logit_cap, student_scale / logit_cap)

    item = lax.axis_index("items")
    rep = lax.axis_index("rep")
    core_id = item % 2
    type_b = item // 2 % 2

    def send(block, move):
        return lax.ppermute(block, AXES, edges(n_items, move))

    def stage(*blocks):
        return lax.optimization_barrier(blocks)

    where = jnp.reshape(rep, (1,)).astype(jnp.int32)
    diag_half = send(gather(where, teacher_items, student_items), diag)
    own = (teacher_items, student_items)
    far_span = [send(block, far) for block in own]
    across = [send(block, cross) for block in own]
    other_tq = send(teacher_queries, core)
    other_sq = send(student_queries, core)

    passes = jnp.arange(teacher_norms.shape[0], dtype=jnp.int32)
    picked = (pass_index[None, :] == passes[:, None]).astype(jnp.float32)
    fold = math.log2(loss_weight * student_scale)
    zt = jnp.sum(teacher_norms * picked, axis=0) * log2e - fold
    zs = jnp.sum(student_norms * picked, axis=0) * log2e - fold
    near = 1 - 2 * core_id
    ahead = 2 - 4 * type_b
    offsets = jnp.stack([0 * near, ahead, -ahead, -3 * near, near, ahead + near, near - ahead])
    reach = block_mask.shape[1] // 2
    chosen = offsets[:, None, None] + reach == jnp.arange(2 * reach + 1)[None, None, :]
    on = jnp.any(chosen & (block_mask[None] != 0), axis=2)
    on = jnp.broadcast_to(on[:, :, None], (on.shape[0], blocks, rows // blocks))
    on = on.reshape(on.shape[0], rows)
    zt_all = jnp.where(on, zt[None], never)
    zs_all = jnp.where(on, zs[None], never)
    other_z = send(jnp.concatenate([zt_all[3:], zs_all[3:]]), core)
    mine = (zt_all, zs_all, *turn(teacher_queries, student_queries), student_queries)
    other = (other_z[:4], other_z[4:], *turn(other_tq, other_sq), other_sq)
    both = (mine, other)
    q, own_term = visit(where, own, (0, 1), (0, 1), both, scales, [])

    diag_half, q, own_term = stage(diag_half, q, own_term)
    next_half = send(diag_half, pair)
    q, diag_term = visit(where, [diag_half], None, (2, 3), both, scales, q, cost=long_cost)
    diag_back = send(diag_term, diag)

    far_span, next_half, q, own_term, diag_back = stage(far_span, next_half, q, own_term, diag_back)
    q[:1], far_term = visit(where, far_span, (0, 1), (3,), both[:1], scales, q[:1])
    pair_back = send(jnp.concatenate([own_term[half:], far_term[half:]]), pair)
    q, next_term = visit(where, [next_half], None, (2, 3), both, scales, q)
    next_back = send(next_term, diag_two)

    across, q, own_term, far_term, next_back = stage(across, q, own_term, far_term, next_back)
    q, first_term = visit(where, across, (1,), (1, 2), both, scales, q)
    cross_back = send(first_term, cross)
    far_back = send(far_term[:half] + pair_back[half:], far)
    q, last_term = visit(where, across, (0,), (1, 2), both, scales, q, cost=long_cost)
    q = q[0] + send(q[1], core)
    last_back = send(last_term, two)
    total = own_term[:half] + pair_back[:half] + diag_back + next_back
    return q.T, total + cross_back + far_back + last_back


def solution(mesh):
    return jax.shard_map(
        shards,
        mesh=mesh,
        in_specs=(
            P(("items", "rep"), None),
            P("items", None),
            P(("items", "rep"), None),
            P("items", None),
            P(("items", "rep"), None),
            P(("items", "rep")),
            P(None, ("items", "rep")),
            P(None, ("items", "rep")),
        ),
        out_specs=(P(("items", "rep"), None), P(("items", "rep"), None)),
        check_vma=False,
    )
```

```python
import functools
import math

import jax
import jax.numpy as jnp
from jax import lax
from jax.experimental import pallas as pl
from jax.experimental.pallas import tpu as pltpu
from jax.sharding import PartitionSpec as P

logit_cap = 10.0
score_gain = 3.0
loss_weight = 8.0
log2e = 1.0 / math.log(2.0)
never = 1e9
long_cost = 10**10
AXES = ("items", "rep")


def edges(n_items, move):
    pairs = []
    for flat in range(n_items * 2):
        item, rep = flat // 2, flat % 2
        pos, y, core = item // 4, (item // 2 % 2) * 2 + rep, item % 2
        pos, y, core = move(pos, y, core)
        pos = pos % (n_items // 4)
        target = ((pos * 2 + y // 2) * 2 + core) * 2 + y % 2
        pairs.append((flat, target))
    return pairs


def step(y):
    return -1 if y < 2 else 1


def far(p, y, c):
    return (p + 1, y, 0) if c == 1 else (p - 1, y, 1)


def cross(p, y, c):
    return p, 3 - y, c


def pair(p, y, c):
    return p, y ^ 1, c


def two(p, y, c):
    return p, y ^ 2, c


def core(p, y, c):
    return p, y, 1 - c


def diag(p, y, c):
    return p + step(y), 3 - y, c


def diag_two(p, y, c):
    return p + step(y), y ^ 2, c


def far_pair(p, y, c):
    p, y, c = far(p, y, c)
    return p, y ^ 1, c


def gather_kernel(parts, rep_ref, teacher_ref, student_ref, *refs):
    *out_refs, sems = refs
    width = teacher_ref.shape[1]
    half = teacher_ref.shape[0] // 2
    copies = []
    for out_ref, (other, skipped) in zip(out_refs, parts, strict=True):
        rows = out_ref.shape[0]
        for first in range(0, rows, half):
            swap = (other or first > 0) != 0
            start = pl.multiple_of((1 - rep_ref[0] if swap else rep_ref[0]) * half, half) + skipped
            count = min(rows, half)
            for source, column in ((teacher_ref, 0), (student_ref, width)):
                target = out_ref.at[pl.ds(first, count), pl.ds(column, source.shape[1])]
                copies.append(
                    pltpu.make_async_copy(source.at[pl.ds(start, count), :], target, sems.at[len(copies)])
                )
    for copy in copies:
        copy.start()
    for copy in copies:
        copy.wait()


def gather(parts, rep, teacher, student):
    width = teacher.shape[1] + student.shape[1]
    whole = pl.BlockSpec(memory_space=pl.ANY)
    return pl.pallas_call(
        functools.partial(gather_kernel, [part[:2] for part in parts]),
        out_shape=[jax.ShapeDtypeStruct((part[2], width), teacher.dtype) for part in parts],
        in_specs=[pl.BlockSpec(memory_space=pltpu.SMEM), whole, whole],
        out_specs=[pl.BlockSpec(memory_space=pltpu.VMEM)] * len(parts),
        scratch_shapes=[pltpu.SemaphoreType.DMA((4 * len(parts),))],
        compiler_params=pltpu.CompilerParams(vmem_limit_bytes=56 << 20),
        cost_estimate=pl.CostEstimate(flops=1, bytes_accessed=1, transcendentals=0),
    )(rep, teacher, student)


def turn_kernel(tq_ref, sq_ref, tqt_ref, sqt_ref):
    rows = 256
    for start in range(0, tq_ref.shape[0], rows):
        tqt_ref[:, start : start + rows] = tq_ref[start : start + rows, :].T
        sqt_ref[:, start : start + rows] = sq_ref[start : start + rows, :].T


def turn(tq, sq):
    vmem = pl.BlockSpec(memory_space=pltpu.VMEM)
    return pl.pallas_call(
        turn_kernel,
        out_shape=tuple(pltpu.VMEM(block.shape[::-1], block.dtype) for block in (tq, sq)),
        in_specs=[vmem] * 2,
        out_specs=(vmem,) * 2,
        compiler_params=pltpu.CompilerParams(vmem_limit_bytes=16 << 20),
        cost_estimate=pl.CostEstimate(flops=1, bytes_accessed=1, transcendentals=0),
    )(tq, sq)


def visit_kernel(pieces, rows, first, scales, *refs):
    groups = len(rows)
    term_ref = refs[-1]
    piece = [ref[...] for ref in refs[:pieces]]
    piece = piece[0] if pieces == 1 else jnp.concatenate(piece)
    refs = refs[pieces:]
    width = piece.shape[1] - term_ref.shape[1]
    teacher, student = piece[:, :width], piece[:, width:]
    term = None
    for group, row in enumerate(rows):
        zt_ref, zs_ref, tqt_ref, sqt_ref, sq_ref = refs[group * 5 : group * 5 + 5]
        t_raw = jnp.dot(teacher, tqt_ref[...], preferred_element_type=jnp.float32)
        s_raw = jnp.dot(student, sqt_ref[...], preferred_element_type=jnp.float32)
        t_tanh = jnp.tanh(t_raw * scales[0])
        s_tanh = jnp.tanh(s_raw * scales[1])
        t_exp = jnp.exp2(t_tanh * (logit_cap * log2e) - zt_ref[row : row + 1, :])
        s_exp = jnp.exp2(s_tanh * (logit_cap * log2e) - zs_ref[row : row + 1, :])
        grads = ((s_exp - t_exp) * (1.0 - s_tanh * s_tanh)).astype(jnp.bfloat16)
        part = jnp.dot(grads, sq_ref[...], preferred_element_type=jnp.float32)
        term = part if term is None else term + part
        q_part = lax.dot_general(
            student, grads, (((0,), (0,)), ((), ())), preferred_element_type=jnp.float32
        )
        q_ref = refs[-1 - groups + group]
        q_ref[...] = q_part if first else refs[groups * 5 + group][...] + q_part
    term_ref[...] = term


def visit(pieces, rows, groups, scales, totals, cost=1):
    width, requests = groups[0][3].shape
    vmem = pl.BlockSpec(memory_space=pltpu.VMEM)
    items = sum(piece.shape[0] for piece in pieces)
    operands = [*pieces]
    for group in groups:
        operands.extend(group)
    operands.extend(totals)
    *totals, term = pl.pallas_call(
        functools.partial(visit_kernel, len(pieces), rows, not totals, scales),
        out_shape=tuple([jax.ShapeDtypeStruct((width, requests), jnp.float32)] * len(groups))
        + (jax.ShapeDtypeStruct((items, width), jnp.float32),),
        in_specs=[vmem] * len(operands),
        out_specs=(vmem,) * (len(groups) + 1),
        compiler_params=pltpu.CompilerParams(vmem_limit_bytes=24 << 20),
        cost_estimate=pl.CostEstimate(flops=cost, bytes_accessed=1, transcendentals=0),
    )(*operands)
    return totals, term


def shards(
    teacher_queries,
    teacher_items,
    student_queries,
    student_items,
    block_mask,
    pass_index,
    teacher_norms,
    student_norms,
):
    n_items = lax.axis_size("items")
    rows = teacher_queries.shape[0]
    blocks = block_mask.shape[0]
    span = teacher_items.shape[0]
    half = span // 2
    quarter = half // 2
    teacher_scale = score_gain / math.sqrt(teacher_queries.shape[1])
    student_scale = score_gain / math.sqrt(student_queries.shape[1])
    scales = (teacher_scale / logit_cap, student_scale / logit_cap)

    item = lax.axis_index("items")
    rep = lax.axis_index("rep")
    core_id = item % 2
    type_b = item // 2 % 2

    def send(block, move):
        return lax.ppermute(block, AXES, edges(n_items, move))

    def stage(*blocks):
        return lax.optimization_barrier(blocks)

    where = jnp.reshape(rep, (1,)).astype(jnp.int32)
    (half_mine,) = gather([(0, 0, half)], where, teacher_items, student_items)
    diag_half = send(half_mine, diag)
    own, tail = gather([(0, 0, span), (1, quarter, quarter)], where, teacher_items, student_items)
    other_tq = send(teacher_queries, core)
    other_sq = send(student_queries, core)

    passes = jnp.arange(teacher_norms.shape[0], dtype=jnp.int32)
    picked = (pass_index[None, :] == passes[:, None]).astype(jnp.float32)
    fold = math.log2(loss_weight * student_scale)
    zt = jnp.sum(teacher_norms * picked, axis=0) * log2e - fold
    zs = jnp.sum(student_norms * picked, axis=0) * log2e - fold
    near = 1 - 2 * core_id
    ahead = 2 - 4 * type_b
    offsets = jnp.stack([0 * near, ahead, -ahead, -3 * near, near, ahead + near, near - ahead])
    reach = block_mask.shape[1] // 2
    chosen = offsets[:, None, None] + reach == jnp.arange(2 * reach + 1)[None, None, :]
    on = jnp.any(chosen & (block_mask[None] != 0), axis=2)
    on = jnp.broadcast_to(on[:, :, None], (on.shape[0], blocks, rows // blocks))
    on = on.reshape(on.shape[0], rows)
    zt_all = jnp.where(on, zt[None], never)
    zs_all = jnp.where(on, zs[None], never)
    other_z = send(jnp.concatenate([zt_all[3:], zs_all[3:]]), core)
    mine = (zt_all, zs_all, *turn(teacher_queries, student_queries), student_queries)
    other = (other_z[:4], other_z[4:], *turn(other_tq, other_sq), other_sq)
    both = (mine, other)
    half_mine, own_too, _ = stage(half_mine, own, other[2])
    cross_half = send(half_mine, cross)
    far_span = send(own_too, far)
    q, own_term = visit([own], (0, 1), both, scales, [])

    diag_half, tail, q, own_term = stage(diag_half, tail, q, own_term)
    next_half = send(diag_half, pair)
    cross_tail = send(tail, cross)
    q, diag_term = visit([diag_half], (2, 3), both, scales, q, cost=long_cost)
    diag_back = send(diag_term, diag)
    far_span, q, own_term = stage(far_span, q, own_term)
    q[:1], far_term = visit([far_span], (3,), both[:1], scales, q[:1], cost=long_cost)
    pair_back = send(jnp.concatenate([own_term[half:], far_term[half:]]), pair)

    cross_half, next_half, q, own_term, far_term, diag_back = stage(
        cross_half, next_half, q, own_term, far_term, diag_back
    )
    cross_head = send(cross_half[:quarter], pair)
    q, next_term = visit([next_half], (2, 3), both, scales, q, cost=long_cost)
    next_back = send(next_term, diag_two)
    q, cross_term = visit([cross_half], (1, 2), both, scales, q, cost=long_cost)
    cross_back = send(cross_term, cross)
    far_back = send(far_term[:half] + pair_back[half:], far)

    cross_head, cross_tail, q, own_term, pair_back = stage(
        cross_head, cross_tail, q, own_term, pair_back
    )
    rest = [cross_head, cross_tail]
    q[1:], other_term = visit(rest, (2,), both[1:], scales, q[1:], cost=long_cost)
    q_back = send(q[1], core)
    q[:1], last_term = visit(rest, (1,), both[:1], scales, q[:1], cost=long_cost)
    last_back = send((last_term + other_term).astype(jnp.bfloat16), two)
    total = own_term[:half] + pair_back[:half] + diag_back + next_back + cross_back + far_back
    q_out, total = stage((q[0] + q_back).T, total)
    return q_out, total + last_back.astype(jnp.float32)


def solution(mesh):
    return jax.shard_map(
        shards,
        mesh=mesh,
        in_specs=(
            P(("items", "rep"), None),
            P("items", None),
            P(("items", "rep"), None),
            P("items", None),
            P(("items", "rep"), None),
            P(("items", "rep")),
            P(None, ("items", "rep")),
            P(None, ("items", "rep")),
        ),
        out_specs=(P(("items", "rep"), None), P(("items", "rep"), None)),
        check_vma=False,
    )
```

```python
import functools
import math

import jax
import jax.numpy as jnp
from jax import lax
from jax.experimental import pallas as pl
from jax.experimental.pallas import tpu as pltpu
from jax.sharding import PartitionSpec as P

logit_cap = 10.0
score_gain = 3.0
loss_weight = 8.0
log2e = 1.0 / math.log(2.0)
never = 1e9
long_cost = 10**10
AXES = ("items", "rep")


def edges(n_items, move):
    pairs = []
    for flat in range(n_items * 2):
        item, rep = flat // 2, flat % 2
        pos, y, core = item // 4, (item // 2 % 2) * 2 + rep, item % 2
        pos, y, core = move(pos, y, core)
        pos = pos % (n_items // 4)
        target = ((pos * 2 + y // 2) * 2 + core) * 2 + y % 2
        pairs.append((flat, target))
    return pairs


def step(y):
    return -1 if y < 2 else 1


def far(p, y, c):
    return (p + 1, y, 0) if c == 1 else (p - 1, y, 1)


def cross(p, y, c):
    return p, 3 - y, c


def pair(p, y, c):
    return p, y ^ 1, c


def two(p, y, c):
    return p, y ^ 2, c


def core(p, y, c):
    return p, y, 1 - c


def diag(p, y, c):
    return p + step(y), 3 - y, c


def diag_two(p, y, c):
    return p + step(y), y ^ 2, c


def far_pair(p, y, c):
    p, y, c = far(p, y, c)
    return p, y ^ 1, c


def gather_kernel(parts, rep_ref, teacher_ref, student_ref, *refs):
    *out_refs, sems = refs
    width = teacher_ref.shape[1]
    half = teacher_ref.shape[0] // 2
    copies = []
    for out_ref, (other, skipped) in zip(out_refs, parts, strict=True):
        rows = out_ref.shape[0]
        for first in range(0, rows, half):
            swap = (other or first > 0) != 0
            start = pl.multiple_of((1 - rep_ref[0] if swap else rep_ref[0]) * half, half) + skipped
            count = min(rows, half)
            for source, column in ((teacher_ref, 0), (student_ref, width)):
                target = out_ref.at[pl.ds(first, count), pl.ds(column, source.shape[1])]
                copies.append(
                    pltpu.make_async_copy(source.at[pl.ds(start, count), :], target, sems.at[len(copies)])
                )
    for copy in copies:
        copy.start()
    for copy in copies:
        copy.wait()


def gather(parts, rep, teacher, student):
    width = teacher.shape[1] + student.shape[1]
    whole = pl.BlockSpec(memory_space=pl.ANY)
    return pl.pallas_call(
        functools.partial(gather_kernel, [part[:2] for part in parts]),
        out_shape=[jax.ShapeDtypeStruct((part[2], width), teacher.dtype) for part in parts],
        in_specs=[pl.BlockSpec(memory_space=pltpu.SMEM), whole, whole],
        out_specs=[pl.BlockSpec(memory_space=pltpu.VMEM)] * len(parts),
        scratch_shapes=[pltpu.SemaphoreType.DMA((4 * len(parts),))],
        compiler_params=pltpu.CompilerParams(vmem_limit_bytes=56 << 20),
        cost_estimate=pl.CostEstimate(flops=1, bytes_accessed=1, transcendentals=0),
    )(rep, teacher, student)


def turn_kernel(tq_ref, sq_ref, tqt_ref, sqt_ref):
    rows = 256
    for start in range(0, tq_ref.shape[0], rows):
        tqt_ref[:, start : start + rows] = tq_ref[start : start + rows, :].T
        sqt_ref[:, start : start + rows] = sq_ref[start : start + rows, :].T


def turn(tq, sq):
    vmem = pl.BlockSpec(memory_space=pltpu.VMEM)
    return pl.pallas_call(
        turn_kernel,
        out_shape=tuple(pltpu.VMEM(block.shape[::-1], block.dtype) for block in (tq, sq)),
        in_specs=[vmem] * 2,
        out_specs=(vmem,) * 2,
        compiler_params=pltpu.CompilerParams(vmem_limit_bytes=16 << 20),
        cost_estimate=pl.CostEstimate(flops=1, bytes_accessed=1, transcendentals=0),
    )(tq, sq)


def visit_kernel(pieces, rows, first, scales, *refs):
    groups = len(rows)
    term_ref = refs[-1]
    piece = [ref[...] for ref in refs[:pieces]]
    piece = piece[0] if pieces == 1 else jnp.concatenate(piece)
    refs = refs[pieces:]
    width = piece.shape[1] - term_ref.shape[1]
    teacher, student = piece[:, :width], piece[:, width:]
    term = None
    for group, row in enumerate(rows):
        zt_ref, zs_ref, tqt_ref, sqt_ref, sq_ref = refs[group * 5 : group * 5 + 5]
        t_raw = jnp.dot(teacher, tqt_ref[...], preferred_element_type=jnp.float32)
        s_raw = jnp.dot(student, sqt_ref[...], preferred_element_type=jnp.float32)
        t_tanh = jnp.tanh(t_raw * scales[0])
        s_tanh = jnp.tanh(s_raw * scales[1])
        t_exp = jnp.exp2(t_tanh * (logit_cap * log2e) - zt_ref[row : row + 1, :])
        s_exp = jnp.exp2(s_tanh * (logit_cap * log2e) - zs_ref[row : row + 1, :])
        grads = ((s_exp - t_exp) * (1.0 - s_tanh * s_tanh)).astype(jnp.bfloat16)
        part = jnp.dot(grads, sq_ref[...], preferred_element_type=jnp.float32)
        term = part if term is None else term + part
        q_part = lax.dot_general(
            student, grads, (((0,), (0,)), ((), ())), preferred_element_type=jnp.float32
        )
        q_ref = refs[-1 - groups + group]
        q_ref[...] = q_part if first else refs[groups * 5 + group][...] + q_part
    term_ref[...] = term


def visit(pieces, rows, groups, scales, totals, cost=1):
    width, requests = groups[0][3].shape
    vmem = pl.BlockSpec(memory_space=pltpu.VMEM)
    items = sum(piece.shape[0] for piece in pieces)
    operands = [*pieces]
    for group in groups:
        operands.extend(group)
    operands.extend(totals)
    *totals, term = pl.pallas_call(
        functools.partial(visit_kernel, len(pieces), rows, not totals, scales),
        out_shape=tuple([jax.ShapeDtypeStruct((width, requests), jnp.float32)] * len(groups))
        + (jax.ShapeDtypeStruct((items, width), jnp.float32),),
        in_specs=[vmem] * len(operands),
        out_specs=(vmem,) * (len(groups) + 1),
        compiler_params=pltpu.CompilerParams(vmem_limit_bytes=24 << 20),
        cost_estimate=pl.CostEstimate(flops=cost, bytes_accessed=1, transcendentals=0),
    )(*operands)
    return totals, term


def shards(
    teacher_queries,
    teacher_items,
    student_queries,
    student_items,
    block_mask,
    pass_index,
    teacher_norms,
    student_norms,
):
    n_items = lax.axis_size("items")
    rows = teacher_queries.shape[0]
    blocks = block_mask.shape[0]
    span = teacher_items.shape[0]
    half = span // 2
    quarter = half // 2
    teacher_scale = score_gain / math.sqrt(teacher_queries.shape[1])
    student_scale = score_gain / math.sqrt(student_queries.shape[1])
    scales = (teacher_scale / logit_cap, student_scale / logit_cap)

    item = lax.axis_index("items")
    rep = lax.axis_index("rep")
    core_id = item % 2
    type_b = item // 2 % 2

    def send(block, move):
        return lax.ppermute(block, AXES, edges(n_items, move))

    def stage(*blocks):
        return lax.optimization_barrier(blocks)

    where = jnp.reshape(rep, (1,)).astype(jnp.int32)
    (half_mine,) = gather([(0, 0, half)], where, teacher_items, student_items)
    diag_half = send(half_mine, diag)
    own, tail = gather([(0, 0, span), (1, quarter, quarter)], where, teacher_items, student_items)
    other_tq = send(teacher_queries, core)
    other_sq = send(student_queries, core)

    passes = jnp.arange(teacher_norms.shape[0], dtype=jnp.int32)
    picked = (pass_index[None, :] == passes[:, None]).astype(jnp.float32)
    fold = math.log2(loss_weight * student_scale)
    zt = jnp.sum(teacher_norms * picked, axis=0) * log2e - fold
    zs = jnp.sum(student_norms * picked, axis=0) * log2e - fold
    near = 1 - 2 * core_id
    ahead = 2 - 4 * type_b
    offsets = jnp.stack([0 * near, ahead, -ahead, -3 * near, near, ahead + near, near - ahead])
    reach = block_mask.shape[1] // 2
    chosen = offsets[:, None, None] + reach == jnp.arange(2 * reach + 1)[None, None, :]
    on = jnp.any(chosen & (block_mask[None] != 0), axis=2)
    on = jnp.broadcast_to(on[:, :, None], (on.shape[0], blocks, rows // blocks))
    on = on.reshape(on.shape[0], rows)
    zt_all = jnp.where(on, zt[None], never)
    zs_all = jnp.where(on, zs[None], never)
    other_z = send(jnp.concatenate([zt_all[3:], zs_all[3:]]), core)
    mine = (zt_all, zs_all, *turn(teacher_queries, student_queries), student_queries)
    other = (other_z[:4], other_z[4:], *turn(other_tq, other_sq), other_sq)
    both = (mine, other)
    half_mine, own_too, _ = stage(half_mine, own, other[2])
    cross_half = send(half_mine, cross)
    far_span = send(own_too, far)
    q, own_term = visit([own], (0, 1), both, scales, [])

    diag_half, tail, q, own_term = stage(diag_half, tail, q, own_term)
    next_half = send(diag_half, pair)
    cross_tail = send(tail, cross)
    q, diag_term = visit([diag_half], (2, 3), both, scales, q, cost=long_cost)
    diag_back = send(diag_term.astype(jnp.bfloat16), diag)
    far_span, q, own_term = stage(far_span, q, own_term)
    q[:1], far_term = visit([far_span], (3,), both[:1], scales, q[:1], cost=long_cost)
    pair_back = send(jnp.concatenate([own_term[half:], far_term[half:]]).astype(jnp.bfloat16), pair)

    cross_half, next_half, q, own_term, far_term, diag_back = stage(
        cross_half, next_half, q, own_term, far_term, diag_back
    )
    cross_head = send(cross_half[:quarter], pair)
    q, next_term = visit([next_half], (2, 3), both, scales, q, cost=long_cost)
    next_back = send(next_term, diag_two)
    q, cross_term = visit([cross_half], (1, 2), both, scales, q, cost=long_cost)
    cross_back = send(cross_term, cross)
    pair_back = pair_back.astype(jnp.float32)
    far_back = send(far_term[:half] + pair_back[half:], far)

    cross_head, cross_tail, q, own_term, pair_back = stage(
        cross_head, cross_tail, q, own_term, pair_back
    )
    rest = [cross_head, cross_tail]
    q[1:], other_term = visit(rest, (2,), both[1:], scales, q[1:], cost=long_cost)
    q_back = send(q[1], core)
    q[:1], last_term = visit(rest, (1,), both[:1], scales, q[:1], cost=long_cost)
    last_back = send((last_term + other_term).astype(jnp.bfloat16), two)
    total = own_term[:half] + pair_back[:half] + next_back + cross_back + far_back
    total = total + diag_back.astype(jnp.float32)
    q_out, total = stage((q[0] + q_back).T, total)
    return q_out, total + last_back.astype(jnp.float32)


def solution(mesh):
    return jax.shard_map(
        shards,
        mesh=mesh,
        in_specs=(
            P(("items", "rep"), None),
            P("items", None),
            P(("items", "rep"), None),
            P("items", None),
            P(("items", "rep"), None),
            P(("items", "rep")),
            P(None, ("items", "rep")),
            P(None, ("items", "rep")),
        ),
        out_specs=(P(("items", "rep"), None), P(("items", "rep"), None)),
        check_vma=False,
    )
```
